256 devices in a mesh: cuts: 32 (over z, y_lo, core), out: 8 (over y_hi, x).
Axes of the slice: x: 4, y: 4 (y_hi: 2, y_lo: 2; y = y_hi * 2 + y_lo), z: 8, core: 2. Of those that a mesh axis runs over, the one named last changes fastest.
Arguments:
- panels: bfloat16 [128, 128, 2, 128], P('out', 'cuts'), may hold values from -0.015625 to 0.015625
- leaf_tables: bfloat16 [512, 2, 64, 2, 128], P('cuts', None, 'out'), may hold values from -4 to 4
- leaf_codes: int32 [128, 128], P('out'), may hold values from 0 to 4095
- branch_table: bfloat16 [384, 2, 128, 128], P('cuts'), may hold values from -0.375 to 0.375
- fetch_list: int32 [32, 32, 2], P('cuts'), may hold values from 0 to 11
- slice_terms: int32 [512, 2], P('cuts'), may hold values from 0 to 63
Outputs:
- amplitudes: float32 [128, 128, 2], P('out', 'cuts')
The draws below stay inside these ranges and needn't reach their ends.
All inputs are finite; a program needn't handle non-finite values.
Results may differ from the reference program's by a relative error of at most 0.0029.
Values may be sent and summed in bfloat16 or wider, within the bound.
No kernel may reach another device: no remote copies, remote signals or barrier semaphores. Data moves between devices by JAX's collectives and lax.ppermute only.
A program may use at most 128 MiB of HBM per device.

```python
import math
import jax
import jax.numpy as jnp
import numpy as np
from jax import lax

R = 128
LEAF = 64
BLOCK = 128
CAP = 2
NBR_DEV = 12
SL_DEV = 16
SLICES = 512
BLOCKS = 128
NBR = 384
SLOTS = 64
N_CUTS = 32


def set_ends(array, rng, low, high):
    index_at = [jax.random.randint(jax.random.fold_in(rng, axis), (), 0, length) for axis, length in enumerate(array.shape)]
    main_axis = array.shape.index(max(array.shape))
    next_to = index_at[:main_axis] + [(index_at[main_axis] + 1) % array.shape[main_axis]] + index_at[main_axis + 1:]
    return array.at[tuple(index_at)].set(low).at[tuple(next_to)].set(high)


def level_of(rng, extent, cuts, least, largest):
    def one(position, shards_of):
        draws = jax.random.uniform(jax.random.fold_in(jax.random.fold_in(rng, 6), position), (shards_of,), jnp.float32, least / len(cuts), largest / len(cuts))
        return jnp.repeat(jnp.exp(draws), extent[position] // shards_of).reshape((-1,) + (1,) * (len(extent) - position - 1))

    loudness = one(*cuts[0])
    for cut in cuts[1:]:
        loudness = loudness * one(*cut)
    return loudness


def rank_table(count, lean):
    portions = [(1 << 20) // math.isqrt(rank ** lean) + 1 for rank in range(1, count + 1)]
    spread = 1 + sum(portions) // (1 << 30)
    return np.cumsum(np.array([max(1, weight // spread) for weight in portions]))


def skewed_ids(rng, shape, count, lean):
    table = rank_table(count, lean)
    ticket = jax.random.randint(jax.random.fold_in(rng, 1), shape, 0, int(table[count - 1]))
    rank = jnp.searchsorted(jnp.asarray(table, jnp.int32), ticket, side="right")
    return jax.random.permutation(jax.random.fold_in(rng, 2), count)[rank].astype(jnp.int32)


def centred(own_key, dims, width, most, shards=(), kind=jnp.bfloat16):
    array = width * jax.random.normal(own_key, dims, jnp.float32)
    if shards:
        array = array * level_of(own_key, dims, shards, -0.22, 0.18)
    return jnp.clip(array, -most, most).astype(kind)


def setup_inputs(seed: int = 0) -> dict:
    key_list = jax.random.split(jax.random.key(seed), 7)
    panels = centred(key_list[0], (BLOCKS, BLOCK, 2, R), (2 * R * SLICES) ** -0.5, 0.015625, ((0, 8), (1, 32)))
    leaf_tables = centred(key_list[1], (SLICES, 2, LEAF, 2, R), 0.7, 4.0, ((0, 32), (2, 8)))
    leaf_codes = set_ends(jax.random.randint(key_list[2], (BLOCKS, BLOCK), 0, LEAF * LEAF), jax.random.fold_in(key_list[2], 1), 0, (LEAF * LEAF) - 1).astype(jnp.int32)
    branch_table = centred(key_list[3], (NBR, 2, R, R), (2 * R) ** -0.5, 0.375, ((0, 32),))
    fetch_list = set_ends(jax.random.randint(key_list[4], (N_CUTS, N_CUTS, CAP), 0, NBR_DEV), jax.random.fold_in(key_list[4], 1), 0, NBR_DEV - 1).astype(jnp.int32)
    slice_terms = set_ends(skewed_ids(key_list[5], (SLICES, 2), SLOTS, 2), jax.random.fold_in(key_list[5], 3), 0, SLOTS - 1).astype(jnp.int32)
    return {"panels": panels, "leaf_tables": leaf_tables, "leaf_codes": leaf_codes, "branch_table": branch_table, "fetch_list": fetch_list, "slice_terms": slice_terms}


def reference(panels, leaf_tables, leaf_codes, branch_table, fetch_list, slice_terms):
    holder = (jnp.arange(SLICES, dtype=jnp.int32) // SL_DEV).astype(jnp.int32)
    source = (slice_terms // CAP).astype(jnp.int32)
    within = (slice_terms % CAP).astype(jnp.int32)
    local_ids = fetch_list[holder[:, None], source, within]
    global_ids = (source * NBR_DEV + local_ids).astype(jnp.int32)
    left_block = branch_table[global_ids[:, 0]].astype(jnp.float32)
    right_block = branch_table[global_ids[:, 1]].astype(jnp.float32)
    real_part = jnp.einsum('sij,sjk->sik', left_block[:, 0], right_block[:, 0]) - jnp.einsum('sij,sjk->sik', left_block[:, 1], right_block[:, 1])
    imag_part = jnp.einsum('sij,sjk->sik', left_block[:, 0], right_block[:, 1]) + jnp.einsum('sij,sjk->sik', left_block[:, 1], right_block[:, 0])
    real_part = real_part.astype(jnp.bfloat16)
    imag_part = imag_part.astype(jnp.bfloat16)
    upper = jnp.concatenate([real_part, imag_part], axis=2)
    lower = jnp.concatenate([-imag_part, real_part], axis=2)
    product_big = jnp.concatenate([upper, lower], axis=1)
    rows_all = BLOCKS * BLOCK
    panel_rows = panels.reshape(rows_all, 2 * R).astype(jnp.float32)
    codes_flat = leaf_codes.reshape(rows_all)
    low_code = (codes_flat % LEAF).astype(jnp.int32)
    high_code = (codes_flat // LEAF).astype(jnp.int32)
    groups = SLICES // 4
    product_groups = product_big.reshape(groups, 4, 2 * R, 2 * R)
    table_groups = leaf_tables.reshape(groups, 4, 2, LEAF, 2, R)

    def one_group(running, inputs):
        product_here, table_here = inputs
        mixed = jnp.einsum('ra,sab->srb', panel_rows, product_here.astype(jnp.float32))
        mixed_re = mixed[:, :, :R]
        mixed_im = mixed[:, :, R:]
        table_here = table_here.astype(jnp.float32)
        low_rows = table_here[:, 0][:, low_code]
        high_rows = table_here[:, 1][:, high_code]
        weight_re = low_rows[:, :, 0] * high_rows[:, :, 0] - low_rows[:, :, 1] * high_rows[:, :, 1]
        weight_im = low_rows[:, :, 0] * high_rows[:, :, 1] + low_rows[:, :, 1] * high_rows[:, :, 0]
        sum_re = jnp.sum(mixed_re * weight_re - mixed_im * weight_im, axis=(0, 2))
        sum_im = jnp.sum(mixed_re * weight_im + mixed_im * weight_re, axis=(0, 2))
        return (running[0] + sum_re, running[1] + sum_im), None

    start_sums = (jnp.zeros((rows_all,), jnp.float32), jnp.zeros((rows_all,), jnp.float32))
    final_sums, _ = lax.scan(one_group, start_sums, (product_groups, table_groups))
    return jnp.stack([final_sums[0], final_sums[1]], axis=-1).reshape(BLOCKS, BLOCK, 2)
```

```python
import jax
import jax.numpy as jnp
from jax import lax
from jax.experimental import pallas as pl
from jax.experimental.pallas import tpu as pltpu
from jax.sharding import Mesh, PartitionSpec as P

BF = jnp.bfloat16
F32 = jnp.float32
CUTS = ("z", "yl", "core")
OUT = ("yh", "x")
SPLIT = 2
ROW_TILE = 512
VMEM = 48 * 1024 * 1024


def swap(a, axis):
    return lax.ppermute(a, axis, [(0, 1), (1, 0)])


def pack_kernel(ids, part, table, send):
    for q in range(send.shape[0] * send.shape[1]):
        send[q // 2, q % 2] = table[ids[q]]


def pack(ids, part, table, takers):
    blocks, _, width, _ = table.shape
    rows = width // 8
    return pl.pallas_call(
        pack_kernel,
        out_shape=jax.ShapeDtypeStruct((takers, 2, 2, rows, width), BF),
        grid_spec=pltpu.PrefetchScalarGridSpec(
            num_scalar_prefetch=2,
            grid=(1,),
            in_specs=[
                pl.BlockSpec((blocks, 2, rows, width), lambda i, ids, part: (0, 0, part[0], 0))
            ],
            out_specs=pl.BlockSpec(
                (takers, 2, 2, rows, width), lambda i, ids, part: (0, 0, 0, 0, 0)
            ),
        ),
        compiler_params=pltpu.CompilerParams(vmem_limit_bytes=VMEM),
        name="pack",
    )(ids, part, table)


def choose_kernel(terms, slots, send):
    peers, slices = send.shape[0], send.shape[1]
    for half in range(SPLIT):
        for s in range(slices):
            for t in range(2):
                block = slots[terms[(half * slices + s) * 2 + t]]
                for p in range(peers // SPLIT):
                    send[half * (peers // SPLIT) + p, s, t] = block


def choose(terms, slots, peers):
    count, _, rows, width = slots.shape
    slices = terms.shape[0] // 2 // SPLIT
    shape = (peers, slices, 2, 2, rows, width)
    return pl.pallas_call(
        choose_kernel,
        out_shape=jax.ShapeDtypeStruct(shape, BF),
        grid_spec=pltpu.PrefetchScalarGridSpec(
            num_scalar_prefetch=1,
            grid=(1,),
            in_specs=[pl.BlockSpec((count, 2, rows, width), lambda i, terms: (0, 0, 0, 0))],
            out_specs=pl.BlockSpec(shape, lambda i, terms: (0, 0, 0, 0, 0, 0)),
        ),
        compiler_params=pltpu.CompilerParams(vmem_limit_bytes=VMEM),
        name="choose",
    )(terms, slots)


def weight_kernel(low, high, leaf, weights):
    width = leaf.shape[3] // 2
    for s in range(leaf.shape[1]):
        table = leaf[:, s].reshape(leaf.shape[0] * leaf.shape[2], 2 * width)
        a = jnp.dot(low[...], table, preferred_element_type=F32)
        b = jnp.dot(high[...], table, preferred_element_type=F32)
        a_re, a_im, b_re, b_im = a[:, :width], a[:, width:], b[:, :width], b[:, width:]
        at = s * 2 * width
        weights[:, at : at + width] = (a_re * b_re - a_im * b_im).astype(BF)
        weights[:, at + width : at + 2 * width] = (a_re * b_im + a_im * b_re).astype(BF)


def weigh(low, high, leaf):
    rows, picks = low.shape
    depth = leaf.shape[1] * leaf.shape[3]
    return pl.pallas_call(
        weight_kernel,
        out_shape=jax.ShapeDtypeStruct((rows, depth), BF),
        grid=(rows // ROW_TILE,),
        in_specs=[
            pl.BlockSpec((ROW_TILE, picks), lambda i: (i, 0)),
            pl.BlockSpec((ROW_TILE, picks), lambda i: (i, 0)),
            pl.BlockSpec(leaf.shape, lambda i: (0, 0, 0, 0)),
        ],
        out_specs=pl.BlockSpec((ROW_TILE, depth), lambda i: (i, 0)),
        compiler_params=pltpu.CompilerParams(vmem_limit_bytes=VMEM),
        cost_estimate=pl.CostEstimate(
            flops=8 * rows * 256 * depth, bytes_accessed=2 * rows * depth, transcendentals=0
        ),
        name="weigh",
    )(low, high, leaf)


def amp_kernel(blocks, weights, panels, amps, product):
    parts, slices, _, _, rows, width = blocks.shape

    @pl.when(pl.program_id(0) == 0)
    def _():
        for s in range(slices):
            f = [
                [blocks[:, s, t, c].reshape(parts * rows, width) for c in range(2)]
                for t in range(2)
            ]
            left = jnp.concatenate(f[0], axis=1)
            right = jnp.concatenate(
                [
                    jnp.concatenate([f[1][0], f[1][1]], axis=1),
                    jnp.concatenate([-f[1][1], f[1][0]], axis=1),
                ],
                axis=0,
            )
            both = jnp.dot(left, right, preferred_element_type=F32).T
            re, im = both[:width].astype(BF), both[width:].astype(BF)
            at = s * 2 * width
            product[at : at + width, :width] = re
            product[at : at + width, width:] = im
            product[at + width : at + 2 * width, :width] = -im
            product[at + width : at + 2 * width, width:] = re

    y = jnp.dot(weights[...], product[...], preferred_element_type=F32)
    p_re = panels[:, :width].astype(F32)
    p_im = panels[:, width:].astype(F32)
    y_re, y_im = y[:, :width], y[:, width:]
    amps[0:1, :] = jnp.sum((p_re * y_re - p_im * y_im).T, axis=0, keepdims=True)
    amps[1:2, :] = jnp.sum((p_re * y_im + p_im * y_re).T, axis=0, keepdims=True)


def amplitudes_of(blocks, weights, panels):
    rows, depth = weights.shape
    width = blocks.shape[-1]
    return pl.pallas_call(
        amp_kernel,
        out_shape=jax.ShapeDtypeStruct((2, rows), F32),
        grid=(rows // ROW_TILE,),
        in_specs=[
            pl.BlockSpec(blocks.shape, lambda i: (0,) * 6),
            pl.BlockSpec((ROW_TILE, depth), lambda i: (i, 0)),
            pl.BlockSpec((ROW_TILE, 2 * width), lambda i: (i, 0)),
        ],
        out_specs=pl.BlockSpec((2, ROW_TILE), lambda i: (0, i)),
        scratch_shapes=[pltpu.VMEM((depth, 2 * width), BF)],
        compiler_params=pltpu.CompilerParams(vmem_limit_bytes=VMEM),
        name="amplitudes",
    )(blocks, weights, panels)


def body(panels, leaf_tables, leaf_codes, branch_table, fetch_list, slice_terms):
    cut_count = lax.axis_size(CUTS)
    peers = lax.axis_size(OUT)
    zs, yls = lax.axis_size("z"), lax.axis_size("yl")
    core, yl, yh = lax.axis_index("core"), lax.axis_index("yl"), lax.axis_index("yh")
    blocks, local_rows, _, width = panels.shape
    own = blocks * local_rows
    states = leaf_tables.shape[2]

    wanted = lax.all_to_all(fetch_list[0], CUTS, 0, 0, tiled=True).reshape(-1)
    part = lax.axis_index(OUT).astype(jnp.int32).reshape(1)
    sent = pack(wanted, part, branch_table, cut_count)
    slots = lax.all_to_all(sent, CUTS, 0, 0, tiled=True)
    slots = slots.reshape((2 * cut_count,) + slots.shape[2:])
    chosen = choose(slice_terms.reshape(-1), slots, peers)
    fetched = lax.all_to_all(chosen, OUT, 0, 0, tiled=True)

    slices = leaf_tables.shape[0] // SPLIT
    leaf = leaf_tables.reshape(SPLIT, 1, slices, 2 * states, 2 * width)
    leaf = jnp.broadcast_to(leaf, (SPLIT, peers // SPLIT) + leaf.shape[2:])
    leaf = leaf.reshape((peers,) + leaf.shape[2:])
    leaf = lax.all_to_all(leaf, OUT, 0, 0, tiled=True)

    rows_here = panels.transpose(1, 0, 2, 3).reshape(own, 2 * width)
    rows_here = jnp.stack([rows_here, swap(rows_here, "yh")])
    other = swap(rows_here, "yl")
    rows_here = jnp.where(
        yl == 0, jnp.stack([rows_here, other]), jnp.stack([other, rows_here])
    )
    rows_here = lax.all_gather(rows_here, "z", axis=0, tiled=True)
    rows_here = rows_here.reshape(-1, 2 * width)
    rows_all = jnp.concatenate([rows_here, swap(rows_here, "core")], axis=0)

    codes = leaf_codes.reshape(blocks, zs, yls, 2, local_rows).transpose(3, 1, 2, 4, 0)
    codes = codes.reshape(2, zs, yls, 1, own)
    codes = jnp.concatenate([codes, swap(codes, "yh")], axis=3)
    codes = jnp.where(core == 0, codes, codes[::-1]).reshape(-1, 1)
    leaf_states = states * peers
    low, high = codes % leaf_states, codes // leaf_states
    low = (low // states) * (2 * states) + low % states
    high = (high // states) * (2 * states) + states + high % states
    column = lax.broadcasted_iota(jnp.int32, (1, 2 * leaf_states), 1)
    low = (low == column).astype(BF)
    high = (high == column).astype(BF)
    weights = weigh(low, high, leaf)

    amps = amplitudes_of(fetched, weights, rows_all)
    amps = amps.reshape(2, 2, zs * yls, 2, own)
    amps = amps[:, 0] + swap(amps[:, 1], "core")
    amps = amps.transpose(1, 2, 0, 3)
    amps = jnp.where(yh == 0, amps, amps[:, ::-1])
    amps = lax.all_to_all(
        amps.reshape(zs * yls * 2, 2 * own), ("z", "yl", "yh"), 0, 0, tiled=True
    )
    amps = jnp.sum(amps, axis=0).reshape(2, local_rows, blocks)
    return amps.transpose(2, 1, 0)


def solution(mesh):
    fine = Mesh(mesh.devices.reshape(8, 2, 2, 2, 4), CUTS + OUT)
    return jax.shard_map(
        body,
        mesh=fine,
        in_specs=(
            P(OUT, CUTS, None, None),
            P(CUTS, None, OUT, None, None),
            P(OUT, None),
            P(CUTS, None, None, None),
            P(CUTS, None, None),
            P(CUTS, None),
        ),
        out_specs=P(OUT, CUTS, None),
        check_vma=False,
    )
```

```python
import jax
import jax.numpy as jnp
from jax import lax
from jax.experimental import pallas as pl
from jax.experimental.pallas import tpu as pltpu
from jax.sharding import Mesh, PartitionSpec as P

BF = jnp.bfloat16
F32 = jnp.float32
CUTS = ("z4", "z2", "z1", "yl", "core")
OUT = ("yh", "x")
PARTS = 8
SPLIT = 2
ROW_TILE = 1024
WEIGHT_TILE = 2048
VMEM = 20 * 1024 * 1024
IN_VMEM = pl.BlockSpec(memory_space=pltpu.VMEM)


def swap(a, axis, bit=1):
    count = lax.axis_size(axis)
    return lax.ppermute(a, axis, [(i, i ^ bit) for i in range(count)])


def pack_kernel(me, part, wanted, table, codes, send, ordered):
    takers, capacity = send.shape[0], send.shape[1]
    for d in range(takers):
        ordered[d : d + 1, :] = codes[pl.ds(d ^ me[1], 1), :]
    for d in range(takers):
        for c in range(capacity):
            send[d, c] = table[wanted[d, c, me[0]]]


def pack(me, part, wanted, table, codes):
    blocks, _, width, _ = table.shape
    rows = width // PARTS
    takers, capacity, _ = wanted.shape
    shape = (takers, capacity, 2, rows, width)
    return pl.pallas_call(
        pack_kernel,
        out_shape=(
            jax.ShapeDtypeStruct(shape, BF),
            jax.ShapeDtypeStruct(codes.shape, codes.dtype),
        ),
        grid_spec=pltpu.PrefetchScalarGridSpec(
            num_scalar_prefetch=2,
            grid=(1,),
            in_specs=[
                pl.BlockSpec(memory_space=pltpu.SMEM),
                pl.BlockSpec((blocks, 2, rows, width), lambda i, me, part: (0, 0, part[0], 0)),
                pl.BlockSpec(codes.shape, lambda i, me, part: (0, 0)),
            ],
            out_specs=(
                pl.BlockSpec(shape, lambda i, me, part: (0, 0, 0, 0, 0)),
                pl.BlockSpec(codes.shape, lambda i, me, part: (0, 0)),
            ),
        ),
        compiler_params=pltpu.CompilerParams(vmem_limit_bytes=VMEM),
        name="pack",
    )(me, part, wanted, pltpu.with_memory_space_constraint(table, pltpu.HBM), codes)


def choose_kernel(terms, half, slots, first_rows, second_rows, *refs):
    kept, given, rows = refs[-3:]
    slices = kept.shape[0]
    for out, first in ((kept, half[0] * slices), (given, (1 - half[0]) * slices)):
        for s in range(slices):
            for t in range(2):
                out[s, t] = slots[terms[(first + s) * 2 + t]]
    count = first_rows.shape[0]
    rows[:count] = first_rows[...]
    rows[count:] = second_rows[...]


def choose(terms, half, slots, first_rows, second_rows, ready):
    shape = (terms.shape[0] // 2 // SPLIT, 2) + slots.shape[1:]
    count, pair = first_rows.shape
    scalars = [pl.BlockSpec(memory_space=pltpu.SMEM)] * 2
    return pl.pallas_call(
        choose_kernel,
        out_shape=(jax.ShapeDtypeStruct(shape, BF),) * 2
        + (jax.ShapeDtypeStruct((2 * count, pair), BF),),
        in_specs=scalars + [IN_VMEM] * 3 + [pl.BlockSpec(memory_space=pl.ANY)] * len(ready),
        out_specs=(IN_VMEM,) * 3,
        compiler_params=pltpu.CompilerParams(vmem_limit_bytes=VMEM),
        name="choose",
    )(terms, half, slots, first_rows, second_rows, *ready)


def weight_kernel(low, high, *refs):
    leaf, weights = refs[:-2], refs[-1]
    halves, slices, _, pair = leaf[0].shape
    width = pair // 2

    def tile(i, carry):
        here = pl.ds(pl.multiple_of(i * WEIGHT_TILE, WEIGHT_TILE), WEIGHT_TILE)
        pick_low, pick_high = low[here, :], high[here, :]
        for s in range(slices):
            table = jnp.concatenate([piece[h, s] for h in range(halves) for piece in leaf], axis=0)
            a = jnp.dot(pick_low, table, preferred_element_type=F32)
            b = jnp.dot(pick_high, table, preferred_element_type=F32)
            a_re, a_im, b_re, b_im = a[:, :width], a[:, width:], b[:, :width], b[:, width:]
            at = s * pair
            weights[here, at : at + width] = (a_re * b_re - a_im * b_im).astype(BF)
            weights[here, at + width : at + pair] = (a_re * b_im + a_im * b_re).astype(BF)
        return carry

    lax.fori_loop(0, low.shape[0] // WEIGHT_TILE, tile, 0)


def weigh(low, high, leaf, chosen):
    rows = low.shape[0]
    depth = leaf[0].shape[1] * leaf[0].shape[3]
    return pl.pallas_call(
        weight_kernel,
        out_shape=pltpu.VMEM((rows, depth), BF),
        in_specs=[IN_VMEM] * (2 + len(leaf)) + [pl.BlockSpec(memory_space=pl.ANY)],
        out_specs=IN_VMEM,
        compiler_params=pltpu.CompilerParams(vmem_limit_bytes=VMEM),
        cost_estimate=pl.CostEstimate(
            flops=8 * rows * 256 * depth, bytes_accessed=2 * rows * depth, transcendentals=0
        ),
        name="weigh",
    )(low, high, *leaf, chosen)


def amp_kernel(me, weights, *refs):
    parts = PARTS
    pieces, refs = refs[:parts], refs[parts:]
    panels, (mine, theirs, blocks, product) = refs[:-4], refs[-4:]
    _, slices, _, _, rows, width = blocks.shape
    for r in range(parts):
        blocks[r ^ me[1]] = pieces[r][...]
    for s in range(slices):
        f = [
            [blocks[:, s, t, c].reshape(parts * rows, width) for c in range(2)] for t in range(2)
        ]
        left = jnp.concatenate(f[0], axis=1)
        right = jnp.concatenate(
            [
                jnp.concatenate([f[1][0], f[1][1]], axis=1),
                jnp.concatenate([-f[1][1], f[1][0]], axis=1),
            ],
            axis=0,
        )
        both = jnp.dot(left, right, preferred_element_type=F32).T
        re, im = both[:width].astype(BF), both[width:].astype(BF)
        at = s * 2 * width
        product[at : at + width, :width] = re
        product[at : at + width, width:] = im
        product[at + width : at + 2 * width, :width] = -im
        product[at + width : at + 2 * width, width:] = re

    lines, each = mine.shape[0], mine.shape[1] // 2
    group = panels[0].shape[0]
    for i in range(weights.shape[0] // ROW_TILE):
        here = slice(i * ROW_TILE, (i + 1) * ROW_TILE)
        y = jnp.dot(weights[here, :], product[...], preferred_element_type=F32)
        there = slice(here.start % group, here.start % group + ROW_TILE)
        p_re = panels[here.start // group][there, :width].astype(F32)
        p_im = panels[here.start // group][there, width:].astype(F32)
        y_re, y_im = y[:, :width], y[:, width:]
        re = jnp.sum((p_re * y_re - p_im * y_im).T, axis=0, keepdims=True)
        im = jnp.sum((p_re * y_im + p_im * y_re).T, axis=0, keepdims=True)
        for k in range(ROW_TILE // each):
            line = here.start // each + k
            amps = theirs if line // lines else mine
            to = pl.ds((line % lines) ^ me[0], 1)
            amps[to, :each] = re[:, k * each : (k + 1) * each]
            amps[to, each:] = im[:, k * each : (k + 1) * each]


def amplitudes_of(me, weights, pieces, panels, each):
    rows, depth = weights.shape
    width = pieces[0].shape[-1]
    return pl.pallas_call(
        amp_kernel,
        out_shape=(jax.ShapeDtypeStruct((rows // each // 2, 2 * each), F32),) * 2,
        in_specs=[pl.BlockSpec(memory_space=pltpu.SMEM)]
        + [IN_VMEM] * (1 + len(pieces) + len(panels)),
        out_specs=(IN_VMEM,) * 2,
        scratch_shapes=[
            pltpu.VMEM((len(pieces),) + pieces[0].shape, BF),
            pltpu.VMEM((depth, 2 * width), BF),
        ],
        compiler_params=pltpu.CompilerParams(vmem_limit_bytes=VMEM),
        name="amplitudes",
    )(me, pltpu.with_memory_space_constraint(weights, pltpu.VMEM), *pieces, *panels)


def body(panels, leaf_tables, leaf_codes, branch_table, fetch_list, slice_terms):
    cut_count = lax.axis_size(CUTS)
    peers = lax.axis_size(OUT)
    yh = lax.axis_index("yh").astype(jnp.int32)
    part = lax.axis_index(OUT).astype(jnp.int32)
    blocks, local_rows, _, width = panels.shape
    own = blocks * local_rows
    states = leaf_tables.shape[2]
    order = ("z1", "yh", "yl", "z4", "z2")

    wanted = fetch_list.transpose(0, 2, 1)
    wanted = jnp.broadcast_to(wanted, (cut_count,) + wanted.shape[1:])
    wanted = lax.all_to_all(wanted, CUTS, 0, 0, tiled=True)
    codes = leaf_codes.reshape(blocks, 2, 2, 2, 2, 2, local_rows).transpose(5, 3, 4, 1, 2, 6, 0)
    codes = codes.reshape(cut_count, own)
    me = [lax.axis_index(CUTS), lax.axis_index(("core", "z1", "yl", "z4", "z2"))]
    sent, codes = pack(
        jnp.stack(me).astype(jnp.int32), part.reshape(1), wanted, branch_table, codes
    )
    slots = lax.all_to_all(sent, CUTS, 0, 0, tiled=True)
    slots = slots.reshape((-1,) + slots.shape[2:])

    slices = leaf_tables.shape[0] // SPLIT
    leaf = leaf_tables.reshape(SPLIT, slices, 2 * states, 2 * width)
    kept = jnp.where(yh == 0, leaf[0], leaf[1])
    given = jnp.where(yh == 0, leaf[1], leaf[0])
    leaf = jnp.stack([kept, swap(given, "yh")])
    leaf = [leaf] + [swap(leaf, "x", bit) for bit in range(1, lax.axis_size("x"))]

    rows_here = panels.transpose(1, 0, 2, 3).reshape(own, 2 * width)
    rows_here = jnp.concatenate(
        [rows_here] + [swap(rows_here, ("z4", "z2"), bit) for bit in range(1, 4)], axis=0
    )
    rows_here = jnp.concatenate([rows_here, swap(rows_here, "yl")], axis=0)
    rows_there = swap(rows_here, "yh")

    codes = codes.reshape(4, 1, cut_count // 4, own)
    codes = jnp.concatenate([codes, swap(codes, "yh")], axis=1).reshape(-1, 1)
    leaf_states = states * peers
    low, high = codes % leaf_states, codes // leaf_states
    low = ((low // states) ^ part) * (2 * states) + low % states
    high = ((high // states) ^ part) * (2 * states) + states + high % states
    column = lax.broadcasted_iota(jnp.int32, (1, 2 * leaf_states), 1)
    low = (low == column).astype(BF)
    high = (high == column).astype(BF)

    kept, given, rows_here = choose(
        slice_terms.reshape(-1),
        yh.reshape(1),
        slots,
        rows_here,
        rows_there,
        (low, high, *leaf),
    )
    got = swap(given, "yh")
    pieces = []
    for piece in (kept, got):
        pieces += [piece] + [swap(piece, "x", bit) for bit in range(1, lax.axis_size("x"))]
    weights = weigh(low, high, leaf, kept)

    rows_here = [rows_here, swap(rows_here, "z1")]
    rows_here = rows_here + [swap(a, "core") for a in rows_here]

    place = jnp.stack([lax.axis_index(order).astype(jnp.int32), part])
    mine, theirs = amplitudes_of(place, weights, pieces, rows_here, own)
    amps = mine + swap(theirs, "core")
    amps = lax.all_to_all(amps, order, 0, 0, tiled=True)
    amps = jnp.sum(amps, axis=0).reshape(2, local_rows, blocks)
    return amps.transpose(2, 1, 0)


def solution(mesh):
    fine = Mesh(mesh.devices.reshape(2, 2, 2, 2, 2, 2, 4), CUTS + OUT)
    return jax.shard_map(
        body,
        mesh=fine,
        in_specs=(
            P(OUT, CUTS, None, None),
            P(CUTS, None, OUT, None, None),
            P(OUT, None),
            P(CUTS, None, None, None),
            P(CUTS, None, None),
            P(CUTS, None),
        ),
        out_specs=P(OUT, CUTS, None),
        check_vma=False,
    )
```

```python
import functools

import jax
import jax.numpy as jnp
from jax import lax
from jax.experimental import pallas as pl
from jax.experimental.pallas import tpu as pltpu
from jax.sharding import Mesh, PartitionSpec as P

BF = jnp.bfloat16
F32 = jnp.float32
CUTS = ("z4", "z2", "z1", "yl", "core")
OUT = ("yh", "x")
PARTS = 8
SPLIT = 2
ROW_TILE = 1024
WEIGHT_TILE = 1024
VMEM = 20 * 1024 * 1024
EARLY = pl.CostEstimate(flops=16_000_000_000, bytes_accessed=0, transcendentals=0)
IN_VMEM = pl.BlockSpec(memory_space=pltpu.VMEM)


def in_hbm(a):
    return pltpu.with_memory_space_constraint(a, pltpu.HBM)


def swap(a, axis, bit=1):
    count = lax.axis_size(axis)
    return lax.ppermute(a, axis, [(i, i ^ bit) for i in range(count)])


def prepare_kernel(at, leaf, codes, kept, given, ordered):
    slices, lines, _ = kept.shape
    slices = slices - 1
    kept[:slices] = leaf[pl.ds(at[0] * slices, slices)]
    given[:slices] = leaf[pl.ds((1 - at[0]) * slices, slices)]
    count = codes.shape[0]
    for d in range(count):
        to = d // 2 + d % 2 * (count // 2)
        ordered[to : to + 1, :] = codes[pl.ds(d ^ at[1], 1), :]
    code = jnp.concatenate([ordered[: count // 2], ordered[count // 2 :]], axis=1)
    states = lines // 2 * PARTS
    both = jnp.concatenate([code % states, code // states], axis=1).astype(F32).astype(BF)
    given[slices] = both
    kept[slices] = both


def prepare(at, leaf, codes):
    slices, lines, pair = leaf.shape
    slices = slices // SPLIT
    return pl.pallas_call(
        prepare_kernel,
        out_shape=(
            jax.ShapeDtypeStruct((slices + 1, lines, pair), BF),
            jax.ShapeDtypeStruct((slices + 1, lines, pair), BF),
        ),
        in_specs=[pl.BlockSpec(memory_space=pltpu.SMEM)] + [IN_VMEM] * 2,
        out_specs=(IN_VMEM,) * 2,
        scratch_shapes=[pltpu.VMEM(codes.shape, codes.dtype)],
        compiler_params=pltpu.CompilerParams(vmem_limit_bytes=VMEM),
        name="prepare",
    )(at, leaf, codes)


def join_kernel(parts, *refs):
    pieces, whole = refs[:parts], refs[-1]
    count = pieces[0].shape[0]
    for i, piece in enumerate(pieces):
        whole[i * count : (i + 1) * count] = piece[...]


def join(pieces, after=(), cost=None):
    shape = (len(pieces) * pieces[0].shape[0],) + pieces[0].shape[1:]
    return pl.pallas_call(
        functools.partial(join_kernel, len(pieces)),
        out_shape=jax.ShapeDtypeStruct(shape, pieces[0].dtype),
        in_specs=[IN_VMEM] * len(pieces) + [pl.BlockSpec(memory_space=pl.ANY)] * len(after),
        out_specs=IN_VMEM,
        compiler_params=pltpu.CompilerParams(vmem_limit_bytes=VMEM),
        cost_estimate=cost,
        name="join",
    )(*pieces, *after)


def pack_kernel(me, part, wanted, table, *refs):
    pieces, (send, rows) = refs[:4], refs[-2:]
    takers, capacity = send.shape[0], send.shape[1]
    for d in range(takers):
        for c in range(capacity):
            send[d, c] = table[wanted[d, c, me[0]]]
    count = pieces[0].shape[0]
    for i, piece in enumerate(pieces):
        rows[i * count : (i + 1) * count] = piece[...]


def pack(me, part, wanted, table, pieces, ready):
    blocks, _, width, _ = table.shape
    rows = width // PARTS
    takers, capacity, _ = wanted.shape
    shape = (takers, capacity, 2, rows, width)
    joined = (len(pieces) * pieces[0].shape[0], pieces[0].shape[1])

    def whole(shape):
        return pl.BlockSpec(shape, lambda i, me, part: (0,) * len(shape))

    return pl.pallas_call(
        pack_kernel,
        out_shape=(jax.ShapeDtypeStruct(shape, BF), jax.ShapeDtypeStruct(joined, BF)),
        grid_spec=pltpu.PrefetchScalarGridSpec(
            num_scalar_prefetch=2,
            grid=(1,),
            in_specs=[
                pl.BlockSpec(memory_space=pltpu.SMEM),
                pl.BlockSpec((blocks, 2, rows, width), lambda i, me, part: (0, 0, part[0], 0)),
            ]
            + [whole(piece.shape) for piece in pieces]
            + [pl.BlockSpec(memory_space=pl.ANY)] * len(ready),
            out_specs=(whole(shape), whole(joined)),
        ),
        compiler_params=pltpu.CompilerParams(vmem_limit_bytes=VMEM),
        name="pack",
    )(me, part, wanted, in_hbm(table), *pieces, *ready)


def choose_kernel(terms, half, slots, first_rows, second_rows, *refs):
    kept, given, rows = refs[-3:]
    slices = kept.shape[0]
    for out, first in ((kept, half[0] * slices), (given, (1 - half[0]) * slices)):
        for s in range(slices):
            for t in range(2):
                out[s, t] = slots[terms[t, first + s]]
    count = first_rows.shape[0]
    rows[:count] = first_rows[...]
    rows[count:] = second_rows[...]


def choose(terms, half, slots, first_rows, second_rows, ready):
    shape = (terms.shape[1] // SPLIT, 2) + slots.shape[1:]
    count, pair = first_rows.shape
    scalars = [pl.BlockSpec(memory_space=pltpu.SMEM)] * 2
    return pl.pallas_call(
        choose_kernel,
        out_shape=(jax.ShapeDtypeStruct(shape, BF),) * 2
        + (jax.ShapeDtypeStruct((2 * count, pair), BF),),
        in_specs=scalars + [IN_VMEM] * 3 + [pl.BlockSpec(memory_space=pl.ANY)] * len(ready),
        out_specs=(IN_VMEM,) * 3,
        compiler_params=pltpu.CompilerParams(vmem_limit_bytes=VMEM),
        name="choose",
    )(terms, half, slots, first_rows, second_rows, *ready)


def weight_kernel(part, *refs):
    leaf, weights = refs[:4], refs[-1]
    halves, slices, lines, pair = leaf[0].shape
    slices = slices - 1
    width = pair // 2
    places = []
    for half in range(halves):
        state = leaf[0][half, slices].astype(F32).astype(jnp.int32)
        count = lines // 2
        place = ((state // count) ^ part[0]) * lines + state % count
        places.append((place[:, :width], place[:, width:] + count))
    row = lax.broadcasted_iota(jnp.int32, (PARTS * lines, width), 0)

    def picks(which, p):
        line = p // 8 * 4 + p % 4
        place = places[p // 4 % 2][which][line : line + 1, :]
        return (place == row).astype(F32).astype(BF).T

    for i in range(weights.shape[0] // WEIGHT_TILE):
        here = slice(i * WEIGHT_TILE, (i + 1) * WEIGHT_TILE)
        tile = range(here.start // width, here.stop // width)
        pick_low = jnp.concatenate([picks(0, p) for p in tile], axis=0)
        pick_high = jnp.concatenate([picks(1, p) for p in tile], axis=0)
        for s in range(slices):
            table = jnp.concatenate([piece[h, s] for h in range(halves) for piece in leaf], axis=0)
            a = jnp.dot(pick_low, table, preferred_element_type=F32)
            b = jnp.dot(pick_high, table, preferred_element_type=F32)
            a_re, a_im, b_re, b_im = a[:, :width], a[:, width:], b[:, :width], b[:, width:]
            at = s * pair
            weights[here, at : at + width] = (a_re * b_re - a_im * b_im).astype(BF)
            weights[here, at + width : at + pair] = (a_re * b_im + a_im * b_re).astype(BF)


def weigh(part, leaf, after):
    halves, slices, lines, pair = leaf[0].shape
    rows = halves * lines * (pair // 2)
    depth = (slices - 1) * pair
    return pl.pallas_call(
        weight_kernel,
        out_shape=pltpu.VMEM((rows, depth), BF),
        in_specs=[pl.BlockSpec(memory_space=pltpu.SMEM)]
        + [IN_VMEM] * len(leaf)
        + [pl.BlockSpec(memory_space=pl.ANY)],
        out_specs=IN_VMEM,
        compiler_params=pltpu.CompilerParams(vmem_limit_bytes=VMEM),
        cost_estimate=pl.CostEstimate(
            flops=8 * rows * 256 * depth, bytes_accessed=2 * rows * depth, transcendentals=0
        ),
        name="weigh",
    )(part, *leaf, after)


def amp_kernel(me, weights, *refs):
    parts = PARTS
    pieces, refs = refs[:parts], refs[parts:]
    panels, (mine, theirs, blocks, product) = refs[:-4], refs[-4:]
    _, slices, _, _, rows, width = blocks.shape
    for r in range(parts):
        blocks[r ^ me[1]] = pieces[r][...]
    for s in range(slices):
        f = [
            [blocks[:, s, t, c].reshape(parts * rows, width) for c in range(2)] for t in range(2)
        ]
        left = jnp.concatenate(f[0], axis=1)
        right = jnp.concatenate(
            [
                jnp.concatenate([f[1][0], f[1][1]], axis=1),
                jnp.concatenate([-f[1][1], f[1][0]], axis=1),
            ],
            axis=0,
        )
        both = jnp.dot(left, right, preferred_element_type=F32).T
        re, im = both[:width].astype(BF), both[width:].astype(BF)
        at = s * 2 * width
        product[at : at + width, :width] = re
        product[at : at + width, width:] = im
        product[at + width : at + 2 * width, :width] = -im
        product[at + width : at + 2 * width, width:] = re

    lines, each = mine.shape[0], mine.shape[1] // 2
    group = panels[0].shape[0]
    for i in range(weights.shape[0] // ROW_TILE):
        here = slice(i * ROW_TILE, (i + 1) * ROW_TILE)
        y = jnp.dot(weights[here, :], product[...], preferred_element_type=F32)
        there = slice(here.start % group, here.start % group + ROW_TILE)
        p_re = panels[here.start // group][there, :width].astype(F32)
        p_im = panels[here.start // group][there, width:].astype(F32)
        y_re, y_im = y[:, :width], y[:, width:]
        re = jnp.sum((p_re * y_re - p_im * y_im).T, axis=0, keepdims=True)
        im = jnp.sum((p_re * y_im + p_im * y_re).T, axis=0, keepdims=True)
        for k in range(ROW_TILE // each):
            line = here.start // each + k
            amps = theirs if line // lines else mine
            to = pl.ds((line % lines) ^ me[0], 1)
            amps[to, :each] = re[:, k * each : (k + 1) * each]
            amps[to, each:] = im[:, k * each : (k + 1) * each]


def amplitudes_of(me, weights, pieces, panels, each):
    rows, depth = weights.shape
    width = pieces[0].shape[-1]
    return pl.pallas_call(
        amp_kernel,
        out_shape=(jax.ShapeDtypeStruct((rows // each // 2, 2 * each), F32),) * 2,
        in_specs=[pl.BlockSpec(memory_space=pltpu.SMEM)]
        + [IN_VMEM] * (1 + len(pieces) + len(panels)),
        out_specs=(IN_VMEM,) * 2,
        scratch_shapes=[
            pltpu.VMEM((len(pieces),) + pieces[0].shape, BF),
            pltpu.VMEM((depth, 2 * width), BF),
        ],
        compiler_params=pltpu.CompilerParams(vmem_limit_bytes=VMEM),
        name="amplitudes",
    )(me, pltpu.with_memory_space_constraint(weights, pltpu.VMEM), *pieces, *panels)


def body(panels, leaf_tables, leaf_codes, branch_table, fetch_list, slice_terms):
    cut_count = lax.axis_size(CUTS)
    peers = lax.axis_size(OUT)
    yh = lax.axis_index("yh").astype(jnp.int32)
    part = lax.axis_index(OUT).astype(jnp.int32)
    blocks, local_rows, _, width = panels.shape
    own = blocks * local_rows
    states = leaf_tables.shape[2]
    order = ("z1", "yh", "yl", "z4", "z2")

    wanted = fetch_list.transpose(0, 2, 1)
    wanted = jnp.broadcast_to(wanted, (cut_count,) + wanted.shape[1:])
    wanted = lax.all_to_all(wanted, CUTS, 0, 0, tiled=True)
    rows_here = panels.transpose(1, 0, 2, 3).reshape(own, 2 * width)
    rows_here = [rows_here] + [swap(rows_here, ("z4", "z2"), bit) for bit in range(1, 4)]
    codes = leaf_codes.reshape(blocks, 2, 2, 2, 2, 2, local_rows).transpose(5, 3, 4, 1, 2, 6, 0)
    at = [yh, lax.axis_index(("core", "z1", "yl", "z4", "z2")).astype(jnp.int32)]
    kept, given = prepare(
        jnp.stack(at),
        leaf_tables.reshape(-1, 2 * states, 2 * width),
        codes.reshape(cut_count, own),
    )
    me = lax.axis_index(CUTS).astype(jnp.int32).reshape(1)
    sent, rows_here = pack(me, part.reshape(1), wanted, branch_table, rows_here, (given,))
    slots = lax.all_to_all(sent, CUTS, 0, 0, tiled=True)
    slots = slots.reshape((-1,) + slots.shape[2:])

    got_leaf = swap(given, "yh")
    leaf = join([kept, got_leaf], cost=EARLY).reshape((-1,) + got_leaf.shape)
    leaf = [leaf] + [swap(leaf, "x", bit) for bit in range(1, lax.axis_size("x"))]
    leaf = [in_hbm(a) for a in leaf]

    rows_here = jnp.concatenate([rows_here, swap(rows_here, "yl")], axis=0)
    rows_there = swap(rows_here, "yh")

    kept, given, rows_here = choose(
        slice_terms.T,
        yh.reshape(1),
        slots,
        in_hbm(rows_here),
        in_hbm(rows_there),
        tuple(leaf),
    )
    got = swap(given, "yh")
    pieces = []
    for piece in (kept, got):
        pieces += [piece] + [swap(piece, "x", bit) for bit in range(1, lax.axis_size("x"))]
    weights = weigh(part.reshape(1), leaf, kept)

    rows_here = [rows_here, swap(rows_here, "z1")]
    rows_here = rows_here + [swap(a, "core") for a in rows_here]

    place = jnp.stack([lax.axis_index(order).astype(jnp.int32), part])
    mine, theirs = amplitudes_of(place, weights, pieces, rows_here, own)
    amps = mine + swap(theirs, "core")
    amps = lax.all_to_all(amps, order, 0, 0, tiled=True)
    amps = jnp.sum(amps, axis=0).reshape(2, local_rows, blocks)
    return amps.transpose(2, 1, 0)


def solution(mesh):
    fine = Mesh(mesh.devices.reshape(2, 2, 2, 2, 2, 2, 4), CUTS + OUT)
    return jax.shard_map(
        body,
        mesh=fine,
        in_specs=(
            P(OUT, CUTS, None, None),
            P(CUTS, None, OUT, None, None),
            P(OUT, None),
            P(CUTS, None, None, None),
            P(CUTS, None, None),
            P(CUTS, None),
        ),
        out_specs=P(OUT, CUTS, None),
        check_vma=False,
    )
```

```python
import functools

import jax
import jax.numpy as jnp
from jax import lax
from jax.experimental import pallas as pl
from jax.experimental.pallas import tpu as pltpu
from jax.sharding import Mesh, PartitionSpec as P

BF = jnp.bfloat16
F32 = jnp.float32
CUTS = ("z4", "z2", "z1", "yl", "core")
OUT = ("yh", "x")
PARTS = 8
SPLIT = 2
ROW_TILE = 1024
WEIGHT_TILE = 1024
VMEM = 20 * 1024 * 1024
EARLY = pl.CostEstimate(flops=16_000_000_000, bytes_accessed=0, transcendentals=0)
IN_VMEM = pl.BlockSpec(memory_space=pltpu.VMEM)


def in_hbm(a):
    return pltpu.with_memory_space_constraint(a, pltpu.HBM)


def swap(a, axis, bit=1):
    count = lax.axis_size(axis)
    return lax.ppermute(a, axis, [(i, i ^ bit) for i in range(count)])


def prepare_kernel(at, leaf, codes, kept, given, ordered):
    slices, lines, _ = kept.shape
    slices = slices - 1
    kept[:slices] = leaf[pl.ds(at[0] * slices, slices)]
    given[:slices] = leaf[pl.ds((1 - at[0]) * slices, slices)]
    count = codes.shape[0]
    for d in range(count):
        to = d // 2 + d % 2 * (count // 2)
        ordered[to : to + 1, :] = codes[pl.ds(d ^ at[1], 1), :]
    code = jnp.concatenate([ordered[: count // 2], ordered[count // 2 :]], axis=1)
    states = lines // 2 * PARTS
    both = jnp.concatenate([code % states, code // states], axis=1).astype(F32).astype(BF)
    given[slices] = both
    kept[slices] = both


def prepare(at, leaf, codes):
    slices, lines, pair = leaf.shape
    slices = slices // SPLIT
    return pl.pallas_call(
        prepare_kernel,
        out_shape=(
            jax.ShapeDtypeStruct((slices + 1, lines, pair), BF),
            jax.ShapeDtypeStruct((slices + 1, lines, pair), BF),
        ),
        in_specs=[pl.BlockSpec(memory_space=pltpu.SMEM)] + [IN_VMEM] * 2,
        out_specs=(IN_VMEM,) * 2,
        scratch_shapes=[pltpu.VMEM(codes.shape, codes.dtype)],
        compiler_params=pltpu.CompilerParams(vmem_limit_bytes=VMEM),
        name="prepare",
    )(at, leaf, codes)


def join_kernel(parts, *refs):
    pieces, whole = refs[:parts], refs[-1]
    count = pieces[0].shape[0]
    for i, piece in enumerate(pieces):
        whole[i * count : (i + 1) * count] = piece[...]


def join(pieces, after=(), cost=None):
    shape = (len(pieces) * pieces[0].shape[0],) + pieces[0].shape[1:]
    return pl.pallas_call(
        functools.partial(join_kernel, len(pieces)),
        out_shape=jax.ShapeDtypeStruct(shape, pieces[0].dtype),
        in_specs=[IN_VMEM] * len(pieces) + [pl.BlockSpec(memory_space=pl.ANY)] * len(after),
        out_specs=IN_VMEM,
        compiler_params=pltpu.CompilerParams(vmem_limit_bytes=VMEM),
        cost_estimate=cost,
        name="join",
    )(*pieces, *after)


def pack_kernel(me, part, wanted, table, *refs):
    pieces, (send, rows) = refs[:4], refs[-2:]
    takers, capacity = send.shape[0], send.shape[1]
    for d in range(takers):
        for c in range(capacity):
            send[d, c] = table[wanted[d, c, me[0]]]
    count = pieces[0].shape[0]
    for i, piece in enumerate(pieces):
        rows[i * count : (i + 1) * count] = piece[...]


def pack(me, part, wanted, table, pieces, ready):
    blocks, _, width, _ = table.shape
    rows = width // PARTS
    takers, capacity, _ = wanted.shape
    shape = (takers, capacity, 2, rows, width)
    joined = (len(pieces) * pieces[0].shape[0], pieces[0].shape[1])

    def whole(shape):
        return pl.BlockSpec(shape, lambda i, me, part: (0,) * len(shape))

    return pl.pallas_call(
        pack_kernel,
        out_shape=(jax.ShapeDtypeStruct(shape, BF), jax.ShapeDtypeStruct(joined, BF)),
        grid_spec=pltpu.PrefetchScalarGridSpec(
            num_scalar_prefetch=2,
            grid=(1,),
            in_specs=[
                pl.BlockSpec(memory_space=pltpu.SMEM),
                pl.BlockSpec((blocks, 2, rows, width), lambda i, me, part: (0, 0, part[0], 0)),
            ]
            + [whole(piece.shape) for piece in pieces]
            + [pl.BlockSpec(memory_space=pl.ANY)] * len(ready),
            out_specs=(whole(shape), whole(joined)),
        ),
        compiler_params=pltpu.CompilerParams(vmem_limit_bytes=VMEM),
        name="pack",
    )(me, part, wanted, in_hbm(table), *pieces, *ready)


def choose_kernel(terms, half, slots, *refs):
    kept, given = refs[-2:]
    slices = kept.shape[0]
    for out, first in ((kept, half[0] * slices), (given, (1 - half[0]) * slices)):
        for s in range(slices):
            for t in range(2):
                out[s, t] = slots[terms[t, first + s]]


def choose(terms, half, slots, ready):
    shape = (terms.shape[1] // SPLIT, 2) + slots.shape[1:]
    return pl.pallas_call(
        choose_kernel,
        out_shape=(jax.ShapeDtypeStruct(shape, BF),) * 2,
        in_specs=[pl.BlockSpec(memory_space=pltpu.SMEM)] * 2
        + [IN_VMEM]
        + [pl.BlockSpec(memory_space=pl.ANY)] * len(ready),
        out_specs=(IN_VMEM,) * 2,
        compiler_params=pltpu.CompilerParams(vmem_limit_bytes=VMEM),
        name="choose",
    )(terms, half, slots, *ready)


def weight_kernel(part, *refs):
    leaf, weights = refs[:4], refs[-1]
    halves, slices, lines, pair = leaf[0].shape
    slices = slices - 1
    width = pair // 2
    places = []
    for half in range(halves):
        state = leaf[0][half, slices].astype(F32).astype(jnp.int32)
        count = lines // 2
        place = ((state // count) ^ part[0]) * lines + state % count
        places.append((place[:, :width], place[:, width:] + count))
    row = lax.broadcasted_iota(jnp.int32, (PARTS * lines, width), 0)

    def picks(which, p):
        line = p // 8 * 4 + p % 4
        place = places[p // 4 % 2][which][line : line + 1, :]
        return (place == row).astype(F32).astype(BF).T

    for i in range(weights.shape[0] // WEIGHT_TILE):
        here = slice(i * WEIGHT_TILE, (i + 1) * WEIGHT_TILE)
        tile = range(here.start // width, here.stop // width)
        pick_low = jnp.concatenate([picks(0, p) for p in tile], axis=0)
        pick_high = jnp.concatenate([picks(1, p) for p in tile], axis=0)
        for s in range(slices):
            table = jnp.concatenate([piece[h, s] for h in range(halves) for piece in leaf], axis=0)
            a = jnp.dot(pick_low, table, preferred_element_type=F32)
            b = jnp.dot(pick_high, table, preferred_element_type=F32)
            a_re, a_im, b_re, b_im = a[:, :width], a[:, width:], b[:, :width], b[:, width:]
            at = s * pair
            weights[here, at : at + width] = (a_re * b_re - a_im * b_im).astype(BF)
            weights[here, at + width : at + pair] = (a_re * b_im + a_im * b_re).astype(BF)


def weigh(part, leaf, after):
    halves, slices, lines, pair = leaf[0].shape
    rows = halves * lines * (pair // 2)
    depth = (slices - 1) * pair
    return pl.pallas_call(
        weight_kernel,
        out_shape=pltpu.VMEM((rows, depth), BF),
        in_specs=[pl.BlockSpec(memory_space=pltpu.SMEM)]
        + [IN_VMEM] * len(leaf)
        + [pl.BlockSpec(memory_space=pl.ANY)],
        out_specs=IN_VMEM,
        compiler_params=pltpu.CompilerParams(vmem_limit_bytes=VMEM),
        cost_estimate=pl.CostEstimate(
            flops=8 * rows * 256 * depth, bytes_accessed=2 * rows * depth, transcendentals=0
        ),
        name="weigh",
    )(part, *leaf, after)


def amp_kernel(me, weights, *refs):
    parts = PARTS
    pieces, refs = refs[:parts], refs[parts:]
    panels, (mine, theirs, blocks, product) = refs[:-4], refs[-4:]
    _, slices, _, _, rows, width = blocks.shape
    for r in range(parts):
        blocks[r ^ me[1]] = pieces[r][...]
    for s in range(slices):
        f = [
            [blocks[:, s, t, c].reshape(parts * rows, width) for c in range(2)] for t in range(2)
        ]
        left = jnp.concatenate(f[0], axis=1)
        right = jnp.concatenate(
            [
                jnp.concatenate([f[1][0], f[1][1]], axis=1),
                jnp.concatenate([-f[1][1], f[1][0]], axis=1),
            ],
            axis=0,
        )
        both = jnp.dot(left, right, preferred_element_type=F32).T
        re, im = both[:width].astype(BF), both[width:].astype(BF)
        at = s * 2 * width
        product[at : at + width, :width] = re
        product[at : at + width, width:] = im
        product[at + width : at + 2 * width, :width] = -im
        product[at + width : at + 2 * width, width:] = re

    lines, each = mine.shape[0], mine.shape[1] // 2
    group = panels[0].shape[0]
    for i in range(weights.shape[0] // ROW_TILE):
        here = slice(i * ROW_TILE, (i + 1) * ROW_TILE)
        y = jnp.dot(weights[here, :], product[...], preferred_element_type=F32)
        there = slice(here.start % group, here.start % group + ROW_TILE)
        p_re = panels[here.start // group][there, :width].astype(F32)
        p_im = panels[here.start // group][there, width:].astype(F32)
        y_re, y_im = y[:, :width], y[:, width:]
        re = jnp.sum((p_re * y_re - p_im * y_im).T, axis=0, keepdims=True)
        im = jnp.sum((p_re * y_im + p_im * y_re).T, axis=0, keepdims=True)
        for k in range(ROW_TILE // each):
            line = here.start // each + k
            amps = theirs if line // lines else mine
            to = pl.ds((line % lines) ^ me[0], 1)
            amps[to, :each] = re[:, k * each : (k + 1) * each]
            amps[to, each:] = im[:, k * each : (k + 1) * each]


def amplitudes_of(me, weights, pieces, panels, each):
    rows, depth = weights.shape
    width = pieces[0].shape[-1]
    return pl.pallas_call(
        amp_kernel,
        out_shape=(jax.ShapeDtypeStruct((rows // each // 2, 2 * each), F32),) * 2,
        in_specs=[pl.BlockSpec(memory_space=pltpu.SMEM)]
        + [IN_VMEM] * (1 + len(pieces) + len(panels)),
        out_specs=(IN_VMEM,) * 2,
        scratch_shapes=[
            pltpu.VMEM((len(pieces),) + pieces[0].shape, BF),
            pltpu.VMEM((depth, 2 * width), BF),
        ],
        compiler_params=pltpu.CompilerParams(vmem_limit_bytes=VMEM),
        name="amplitudes",
    )(me, pltpu.with_memory_space_constraint(weights, pltpu.VMEM), *pieces, *panels)


def body(panels, leaf_tables, leaf_codes, branch_table, fetch_list, slice_terms):
    cut_count = lax.axis_size(CUTS)
    peers = lax.axis_size(OUT)
    yh = lax.axis_index("yh").astype(jnp.int32)
    part = lax.axis_index(OUT).astype(jnp.int32)
    blocks, local_rows, _, width = panels.shape
    own = blocks * local_rows
    states = leaf_tables.shape[2]
    order = ("z1", "yh", "yl", "z4", "z2")

    wanted = fetch_list.transpose(0, 2, 1)
    wanted = jnp.broadcast_to(wanted, (cut_count,) + wanted.shape[1:])
    wanted = lax.all_to_all(wanted, CUTS, 0, 0, tiled=True)
    rows_here = panels.transpose(1, 0, 2, 3).reshape(own, 2 * width)
    rows_here = [rows_here] + [swap(rows_here, ("z4", "z2"), bit) for bit in range(1, 4)]
    codes = leaf_codes.reshape(blocks, 2, 2, 2, 2, 2, local_rows).transpose(5, 3, 4, 1, 2, 6, 0)
    at = [yh, lax.axis_index(("core", "z1", "yl", "z4", "z2")).astype(jnp.int32)]
    kept, given = prepare(
        jnp.stack(at),
        leaf_tables.reshape(-1, 2 * states, 2 * width),
        codes.reshape(cut_count, own),
    )
    me = lax.axis_index(CUTS).astype(jnp.int32).reshape(1)
    sent, rows_here = pack(me, part.reshape(1), wanted, branch_table, rows_here, (given,))
    slots = lax.all_to_all(sent, CUTS, 0, 0, tiled=True)
    slots = slots.reshape((-1,) + slots.shape[2:])

    got_leaf = swap(given, "yh")
    leaf = join([kept, got_leaf], cost=EARLY).reshape((-1,) + got_leaf.shape)
    leaf = [leaf] + [swap(leaf, "x", bit) for bit in range(1, lax.axis_size("x"))]
    leaf = [in_hbm(a) for a in leaf]

    rows_here = join([rows_here, swap(rows_here, "yl")])

    kept, given = choose(slice_terms.T, yh.reshape(1), slots, tuple(leaf))
    got = swap(given, "yh")
    pieces = []
    for piece in (kept, got):
        pieces += [piece] + [swap(piece, "x", bit) for bit in range(1, lax.axis_size("x"))]
    weights = weigh(part.reshape(1), leaf, kept)

    rows_here = join([rows_here, swap(rows_here, "yh")], (kept,))
    rows_here = [rows_here, swap(rows_here, "z1")]
    rows_here = rows_here + [swap(a, "core") for a in rows_here]

    place = jnp.stack([lax.axis_index(order).astype(jnp.int32), part])
    mine, theirs = amplitudes_of(place, weights, pieces, rows_here, own)
    amps = mine + swap(theirs, "core")
    amps = lax.all_to_all(amps, order, 0, 0, tiled=True)
    amps = jnp.sum(amps, axis=0).reshape(2, local_rows, blocks)
    return amps.transpose(2, 1, 0)


def solution(mesh):
    fine = Mesh(mesh.devices.reshape(2, 2, 2, 2, 2, 2, 4), CUTS + OUT)
    return jax.shard_map(
        body,
        mesh=fine,
        in_specs=(
            P(OUT, CUTS, None, None),
            P(CUTS, None, OUT, None, None),
            P(OUT, None),
            P(CUTS, None, None, None),
            P(CUTS, None, None),
            P(CUTS, None),
        ),
        out_specs=P(OUT, CUTS, None),
        check_vma=False,
    )
```

```python
import functools

import jax
import jax.numpy as jnp
from jax import lax
from jax.experimental import pallas as pl
from jax.experimental.pallas import tpu as pltpu
from jax.sharding import Mesh, PartitionSpec as P

BF = jnp.bfloat16
F32 = jnp.float32
CUTS = ("z4", "z2", "z1", "yl", "core")
OUT = ("yh", "x")
PARTS = 8
SPLIT = 2
ROW_TILE = 1024
WEIGHT_TILE = 1024
VMEM = 20 * 1024 * 1024
EARLY = pl.CostEstimate(flops=16_000_000_000, bytes_accessed=0, transcendentals=0)
IN_VMEM = pl.BlockSpec(memory_space=pltpu.VMEM)


def in_hbm(a):
    return pltpu.with_memory_space_constraint(a, pltpu.HBM)


def swap(a, axis, bit=1):
    count = lax.axis_size(axis)
    return lax.ppermute(a, axis, [(i, i ^ bit) for i in range(count)])


def repeat_kernel(lists, send):
    for d in range(send.shape[0]):
        send[d] = lists[...]


def repeat(lists, count):
    return pl.pallas_call(
        repeat_kernel,
        out_shape=jax.ShapeDtypeStruct((count,) + lists.shape, lists.dtype),
        in_specs=[IN_VMEM],
        out_specs=IN_VMEM,
        compiler_params=pltpu.CompilerParams(vmem_limit_bytes=VMEM),
        name="repeat",
    )(lists)


def prepare_kernel(at, leaf, codes, kept, given, ordered):
    slices, lines, _ = kept.shape
    slices = slices - 1
    kept[:slices] = leaf[pl.ds(at[0] * slices, slices)]
    given[:slices] = leaf[pl.ds((1 - at[0]) * slices, slices)]
    count = codes.shape[0]
    for d in range(count):
        to = d // 2 + d % 2 * (count // 2)
        ordered[to : to + 1, :] = codes[pl.ds(d ^ at[1], 1), :]
    code = jnp.concatenate([ordered[: count // 2], ordered[count // 2 :]], axis=1)
    states = lines // 2 * PARTS
    both = jnp.concatenate([code % states, code // states], axis=1).astype(F32).astype(BF)
    given[slices] = both
    kept[slices] = both


def prepare(at, leaf, codes):
    slices, lines, pair = leaf.shape
    slices = slices // SPLIT
    return pl.pallas_call(
        prepare_kernel,
        out_shape=(
            jax.ShapeDtypeStruct((slices + 1, lines, pair), BF),
            jax.ShapeDtypeStruct((slices + 1, lines, pair), BF),
        ),
        in_specs=[pl.BlockSpec(memory_space=pltpu.SMEM)] + [IN_VMEM] * 2,
        out_specs=(IN_VMEM,) * 2,
        scratch_shapes=[pltpu.VMEM(codes.shape, codes.dtype)],
        compiler_params=pltpu.CompilerParams(vmem_limit_bytes=VMEM),
        name="prepare",
    )(at, leaf, codes)


def join_kernel(parts, *refs):
    pieces, whole = refs[:parts], refs[-1]
    count = pieces[0].shape[0]
    for i, piece in enumerate(pieces):
        whole[i * count : (i + 1) * count] = piece[...]


def join(pieces, after=(), cost=None):
    shape = (len(pieces) * pieces[0].shape[0],) + pieces[0].shape[1:]
    return pl.pallas_call(
        functools.partial(join_kernel, len(pieces)),
        out_shape=jax.ShapeDtypeStruct(shape, pieces[0].dtype),
        in_specs=[IN_VMEM] * len(pieces) + [pl.BlockSpec(memory_space=pl.ANY)] * len(after),
        out_specs=IN_VMEM,
        compiler_params=pltpu.CompilerParams(vmem_limit_bytes=VMEM),
        cost_estimate=cost,
        name="join",
    )(*pieces, *after)


def pack_kernel(me, part, wanted, table, *refs):
    pieces, (send, rows) = refs[:4], refs[-2:]
    takers, capacity = send.shape[0], send.shape[1]
    for d in range(takers):
        for c in range(capacity):
            send[d, c] = table[wanted[d, c, me[0]]]
    count = pieces[0].shape[0]
    for i, piece in enumerate(pieces):
        rows[i * count : (i + 1) * count] = piece[...]


def pack(me, part, wanted, table, pieces, ready):
    blocks, _, width, _ = table.shape
    rows = width // PARTS
    takers, capacity, _ = wanted.shape
    shape = (takers, capacity, 2, rows, width)
    joined = (len(pieces) * pieces[0].shape[0], pieces[0].shape[1])

    def whole(shape):
        return pl.BlockSpec(shape, lambda i, me, part: (0,) * len(shape))

    return pl.pallas_call(
        pack_kernel,
        out_shape=(jax.ShapeDtypeStruct(shape, BF), jax.ShapeDtypeStruct(joined, BF)),
        grid_spec=pltpu.PrefetchScalarGridSpec(
            num_scalar_prefetch=2,
            grid=(1,),
            in_specs=[
                pl.BlockSpec(memory_space=pltpu.SMEM),
                pl.BlockSpec((blocks, 2, rows, width), lambda i, me, part: (0, 0, part[0], 0)),
            ]
            + [whole(piece.shape) for piece in pieces]
            + [pl.BlockSpec(memory_space=pl.ANY)] * len(ready),
            out_specs=(whole(shape), whole(joined)),
        ),
        compiler_params=pltpu.CompilerParams(vmem_limit_bytes=VMEM),
        name="pack",
    )(me, part, wanted, in_hbm(table), *pieces, *ready)


def choose_kernel(terms, half, slots, *refs):
    kept, given = refs[-2:]
    slices = kept.shape[0]
    for out, first in ((kept, half[0] * slices), (given, (1 - half[0]) * slices)):
        for s in range(slices):
            for t in range(2):
                out[s, t] = slots[terms[t, first + s]]


def choose(terms, half, slots, ready):
    shape = (terms.shape[1] // SPLIT, 2) + slots.shape[1:]
    return pl.pallas_call(
        choose_kernel,
        out_shape=(jax.ShapeDtypeStruct(shape, BF),) * 2,
        in_specs=[pl.BlockSpec(memory_space=pltpu.SMEM)] * 2
        + [IN_VMEM]
        + [pl.BlockSpec(memory_space=pl.ANY)] * len(ready),
        out_specs=(IN_VMEM,) * 2,
        compiler_params=pltpu.CompilerParams(vmem_limit_bytes=VMEM),
        name="choose",
    )(terms, half, slots, *ready)


def weight_kernel(part, *refs):
    leaf, weights = refs[:4], refs[-1]
    halves, slices, lines, pair = leaf[0].shape
    slices = slices - 1
    width = pair // 2
    places = []
    for half in range(halves):
        state = leaf[0][half, slices].astype(F32).astype(jnp.int32)
        count = lines // 2
        place = ((state // count) ^ part[0]) * lines + state % count
        places.append((place[:, :width], place[:, width:] + count))
    row = lax.broadcasted_iota(jnp.int32, (PARTS * lines, width), 0)

    def picks(which, p):
        line = p // 8 * 4 + p % 4
        place = places[p // 4 % 2][which][line : line + 1, :]
        return (place == row).astype(F32).astype(BF).T

    for i in range(weights.shape[0] // WEIGHT_TILE):
        here = slice(i * WEIGHT_TILE, (i + 1) * WEIGHT_TILE)
        tile = range(here.start // width, here.stop // width)
        pick_low = jnp.concatenate([picks(0, p) for p in tile], axis=0)
        pick_high = jnp.concatenate([picks(1, p) for p in tile], axis=0)
        for s in range(slices):
            table = jnp.concatenate([piece[h, s] for h in range(halves) for piece in leaf], axis=0)
            a = jnp.dot(pick_low, table, preferred_element_type=F32)
            b = jnp.dot(pick_high, table, preferred_element_type=F32)
            a_re, a_im, b_re, b_im = a[:, :width], a[:, width:], b[:, :width], b[:, width:]
            at = s * pair
            weights[here, at : at + width] = (a_re * b_re - a_im * b_im).astype(BF)
            weights[here, at + width : at + pair] = (a_re * b_im + a_im * b_re).astype(BF)


def weigh(part, leaf, after):
    halves, slices, lines, pair = leaf[0].shape
    rows = halves * lines * (pair // 2)
    depth = (slices - 1) * pair
    return pl.pallas_call(
        weight_kernel,
        out_shape=pltpu.VMEM((rows, depth), BF),
        in_specs=[pl.BlockSpec(memory_space=pltpu.SMEM)]
        + [IN_VMEM] * len(leaf)
        + [pl.BlockSpec(memory_space=pl.ANY)],
        out_specs=IN_VMEM,
        compiler_params=pltpu.CompilerParams(vmem_limit_bytes=VMEM),
        cost_estimate=pl.CostEstimate(
            flops=8 * rows * 256 * depth, bytes_accessed=2 * rows * depth, transcendentals=0
        ),
        name="weigh",
    )(part, *leaf, after)


def amp_kernel(me, weights, *refs):
    parts = PARTS
    pieces, refs = refs[:parts], refs[parts:]
    panels, (mine, theirs, blocks, product) = refs[:-4], refs[-4:]
    _, slices, _, _, rows, width = blocks.shape
    for r in range(parts):
        blocks[r ^ me[1]] = pieces[r][...]
    for s in range(slices):
        f = [
            [blocks[:, s, t, c].reshape(parts * rows, width) for c in range(2)] for t in range(2)
        ]
        left = jnp.concatenate(f[0], axis=1)
        right = jnp.concatenate(
            [
                jnp.concatenate([f[1][0], f[1][1]], axis=1),
                jnp.concatenate([-f[1][1], f[1][0]], axis=1),
            ],
            axis=0,
        )
        both = jnp.dot(left, right, preferred_element_type=F32).T
        re, im = both[:width].astype(BF), both[width:].astype(BF)
        at = s * 2 * width
        product[at : at + width, :width] = re
        product[at : at + width, width:] = im
        product[at + width : at + 2 * width, :width] = -im
        product[at + width : at + 2 * width, width:] = re

    lines, each = mine.shape[0], mine.shape[1] // 2
    group = panels[0].shape[0]
    for i in range(weights.shape[0] // ROW_TILE):
        here = slice(i * ROW_TILE, (i + 1) * ROW_TILE)
        y = jnp.dot(weights[here, :], product[...], preferred_element_type=F32)
        there = slice(here.start % group, here.start % group + ROW_TILE)
        p_re = panels[here.start // group][there, :width].astype(F32)
        p_im = panels[here.start // group][there, width:].astype(F32)
        y_re, y_im = y[:, :width], y[:, width:]
        re = jnp.sum((p_re * y_re - p_im * y_im).T, axis=0, keepdims=True)
        im = jnp.sum((p_re * y_im + p_im * y_re).T, axis=0, keepdims=True)
        for k in range(ROW_TILE // each):
            line = here.start // each + k
            amps = theirs if line // lines else mine
            to = pl.ds((line % lines) ^ me[0], 1)
            amps[to, :each] = re[:, k * each : (k + 1) * each]
            amps[to, each:] = im[:, k * each : (k + 1) * each]


def amplitudes_of(me, weights, pieces, panels, each):
    rows, depth = weights.shape
    width = pieces[0].shape[-1]
    return pl.pallas_call(
        amp_kernel,
        out_shape=(jax.ShapeDtypeStruct((rows // each // 2, 2 * each), F32),) * 2,
        in_specs=[pl.BlockSpec(memory_space=pltpu.SMEM)]
        + [IN_VMEM] * (1 + len(pieces) + len(panels)),
        out_specs=(IN_VMEM,) * 2,
        scratch_shapes=[
            pltpu.VMEM((len(pieces),) + pieces[0].shape, BF),
            pltpu.VMEM((depth, 2 * width), BF),
        ],
        compiler_params=pltpu.CompilerParams(vmem_limit_bytes=VMEM),
        name="amplitudes",
    )(me, pltpu.with_memory_space_constraint(weights, pltpu.VMEM), *pieces, *panels)


def body(panels, leaf_tables, leaf_codes, branch_table, fetch_list, slice_terms):
    cut_count = lax.axis_size(CUTS)
    peers = lax.axis_size(OUT)
    yh = lax.axis_index("yh").astype(jnp.int32)
    part = lax.axis_index(OUT).astype(jnp.int32)
    blocks, local_rows, _, width = panels.shape
    own = blocks * local_rows
    states = leaf_tables.shape[2]
    order = ("z1", "yh", "yl", "z4", "z2")

    wanted = repeat(fetch_list.transpose(0, 2, 1)[0], cut_count)
    wanted = lax.all_to_all(wanted, CUTS, 0, 0, tiled=True)
    rows_here = panels.transpose(1, 0, 2, 3).reshape(own, 2 * width)
    rows_here = [rows_here] + [swap(rows_here, ("z4", "z2"), bit) for bit in range(1, 4)]
    codes = leaf_codes.reshape(blocks, 2, 2, 2, 2, 2, local_rows).transpose(5, 3, 4, 1, 2, 6, 0)
    at = [yh, lax.axis_index(("core", "z1", "yl", "z4", "z2")).astype(jnp.int32)]
    kept, given = prepare(
        jnp.stack(at),
        leaf_tables.reshape(-1, 2 * states, 2 * width),
        codes.reshape(cut_count, own),
    )
    me = lax.axis_index(CUTS).astype(jnp.int32).reshape(1)
    sent, rows_here = pack(me, part.reshape(1), wanted, branch_table, rows_here, (given,))
    slots = lax.all_to_all(sent, CUTS, 0, 0, tiled=True)
    slots = slots.reshape((-1,) + slots.shape[2:])

    got_leaf = swap(given, "yh")
    leaf = join([kept, got_leaf], cost=EARLY).reshape((-1,) + got_leaf.shape)
    leaf = [leaf] + [swap(leaf, "x", bit) for bit in range(1, lax.axis_size("x"))]
    leaf = [in_hbm(a) for a in leaf]

    rows_here = join([rows_here, swap(rows_here, "yl")])

    kept, given = choose(slice_terms.T, yh.reshape(1), slots, tuple(leaf))
    got = swap(given, "yh")
    pieces = []
    for piece in (kept, got):
        pieces += [piece] + [swap(piece, "x", bit) for bit in range(1, lax.axis_size("x"))]
    weights = weigh(part.reshape(1), leaf, kept)

    rows_here = join([rows_here, swap(rows_here, "yh")], (kept,))
    rows_here = [rows_here, swap(rows_here, "z1")]
    rows_here = rows_here + [swap(a, "core") for a in rows_here]

    place = jnp.stack([lax.axis_index(order).astype(jnp.int32), part])
    mine, theirs = amplitudes_of(place, weights, pieces, rows_here, own)
    amps = mine + swap(theirs, "core")
    amps = lax.all_to_all(amps, order, 0, 0, tiled=True)
    amps = jnp.sum(amps, axis=0).reshape(2, local_rows, blocks)
    return amps.transpose(2, 1, 0)


def solution(mesh):
    fine = Mesh(mesh.devices.reshape(2, 2, 2, 2, 2, 2, 4), CUTS + OUT)
    return jax.shard_map(
        body,
        mesh=fine,
        in_specs=(
            P(OUT, CUTS, None, None),
            P(CUTS, None, OUT, None, None),
            P(OUT, None),
            P(CUTS, None, None, None),
            P(CUTS, None, None),
            P(CUTS, None),
        ),
        out_specs=P(OUT, CUTS, None),
        check_vma=False,
    )
```
